128 devices in a mesh: dp: 8 (over x, core), table: 16 (over y, z).
Axes of the slice: x: 4, y: 4, z: 4, core: 2. Of those that a mesh axis runs over, the one named last changes fastest.
Arguments:
- grad_out: bfloat16 [32768, 4096], P(('dp', 'table')), may hold values from -6 to 6
- slot_weight: float32 [32768, 32], P(('dp', 'table')), may hold values from 0.05 to 1
- slot_pos: int32 [32768, 32], P(('dp', 'table')), may hold values from 0 to 511, as said below
- slot_rows: int32 [16, 128, 32], P('table'), may hold values from 0 to 1023
- values: float32 [16384, 4096], P('table', 'dp'), may hold values from -6 to 6
- first_moment: float32 [16384, 4096], P('table', 'dp'), may hold values from -4 to 4
- second_moment: float32 [16384, 4096], P('table', 'dp'), may hold values from 0.01 to 1
- row_steps: int32 [16384], P('table'), may hold values from 1 to 64
- queries: bfloat16 [32768, 2, 256], P(('dp', 'table')), may hold values from -6 to 6
- score_grad: bfloat16 [32768, 2, 4096], P(('dp', 'table')), may hold values from -0.03125 to 0.03125
Outputs:
- new_values: float32 [16384, 4096], P('table', 'dp')
- new_first: float32 [16384, 4096], P('table', 'dp')
- new_second: float32 [16384, 4096], P('table', 'dp')
- subkey_grad: bfloat16 [2, 4096, 256], replicated
The draws below stay inside these ranges and needn't reach their ends.
Inputs may be any that keep to these rules, and one draw needn't show every extreme that they name: `slot_pos`: three owners drawn from the seed receive some three times the mean share of slots.
All inputs are finite; a program needn't handle non-finite values.
Results may differ from the reference program's by a relative error of at most 0.0058.
Values may be sent and summed in bfloat16 or wider, within the bound.
No kernel may reach another device: no remote copies, remote signals or barrier semaphores. Data moves between devices by JAX's collectives and lax.ppermute only.
A program may use at most 128 MiB of HBM per device.

```python
import math
import jax
import jax.numpy as jnp
from jax import lax

D = 4096
K = 32
NSUB = 4096
KD = 256
TOK_DEV = 256
CAP = 32
R_OWN = 1024
TOKENS = 32768
TOUCHED = 16384
N_TABLE = 16
DEVICES = 128


def draw_slot_pos(key, part):
    key = jax.random.fold_in(key, 7)
    first, second, third, fourth = jax.random.split(key, 4)
    total = N_TABLE * CAP
    spread = jax.random.randint(first, (TOKENS, K), 0, total)
    offset = jax.random.randint(second, (), 0, N_TABLE - 2)
    hotter = jax.random.randint(third, (TOKENS, K), 0, 3 * CAP) + offset * CAP
    pick = jax.random.randint(fourth, (TOKENS, K), 0, 2)
    chosen = jnp.where(pick == 1, hotter, spread).astype(jnp.int32)
    chosen = chosen.at[0, 0].set(0)
    chosen = chosen.at[TOKENS - 1, K - 1].set(total - 1)
    return chosen


def set_ends(values, own_key, low, largest):
    longest = values.shape.index(max(values.shape))
    spots = []
    for shift in (0, 1):
        where = [jax.random.randint(jax.random.fold_in(own_key, axis), (), 0, length) for axis, length in enumerate(values.shape)]
        where[longest] = (where[longest] + shift) % values.shape[longest]
        spots.append(tuple(where))
    return values.at[spots[0]].set(low).at[spots[1]].set(largest)


def level_of(rng, dims, cuts, low, top_value):
    gain, own = 1.0, jax.random.fold_in(rng, 6)
    for axis_at, blocks in cuts:
        draws = jnp.exp(jax.random.uniform(jax.random.fold_in(own, axis_at), (blocks,), jnp.float32, low / len(cuts), top_value / len(cuts)))
        gain = gain * jnp.repeat(draws, dims[axis_at] // blocks).reshape([-1 if axis == axis_at else 1 for axis in range(len(dims))])
    return gain


def noise(key, extent, scale, bound, pieces=(), kind=jnp.bfloat16):
    result = jax.random.normal(key, extent, jnp.float32) * scale
    if len(pieces) > 0:
        result = level_of(key, extent, pieces, -0.22, 0.18) * result
    return jnp.clip(result, min=-bound, max=bound).astype(kind)


def setup_inputs(seed: int = 0) -> dict:
    keys = jax.random.split(jax.random.key(seed), 11)
    grad_out = noise(keys[0], (TOKENS, D), 1.0, 6.0, ((0, 128),))
    slot_weight = jnp.clip(jnp.exp(math.log(1.0) - 2.9957323 * jax.random.uniform(keys[1], (TOKENS, K), jnp.float32) ** level_of(keys[1], (TOKENS, K), ((0, 128),), -0.2, 0.2)), 0.05, 1.0)
    slot_pos = draw_slot_pos(jax.random.fold_in(keys[10], 71), 0)
    slot_rows = set_ends(jax.random.randint(keys[3], (N_TABLE, DEVICES, CAP), 0, R_OWN), jax.random.fold_in(keys[3], 1), 0, R_OWN - 1).astype(jnp.int32)
    values = noise(keys[4], (TOUCHED, D), 1.0, 6.0, ((0, 16), (1, 8)), jnp.float32)
    first_moment = noise(keys[5], (TOUCHED, D), 0.5, 4.0, ((0, 16), (1, 8)), jnp.float32)
    second_moment = jnp.clip(jnp.exp(math.log(1.0) - 4.6051702 * jax.random.uniform(keys[6], (TOUCHED, D), jnp.float32) ** level_of(keys[6], (TOUCHED, D), ((0, 16), (1, 8)), -0.2, 0.2)), 0.01, 1.0)
    row_steps = set_ends(jax.random.randint(keys[7], (TOUCHED,), 1, 65), jax.random.fold_in(keys[7], 1), 1, 64).astype(jnp.int32)
    queries = noise(keys[8], (TOKENS, 2, KD), 1.0, 6.0, ((0, 128),))
    score_grad = noise(keys[9], (TOKENS, 2, NSUB), TOKENS ** -0.5, 0.03125, ((0, 128),))
    return dict(grad_out=grad_out, slot_weight=slot_weight, slot_pos=slot_pos, slot_rows=slot_rows, values=values, first_moment=first_moment, second_moment=second_moment, row_steps=row_steps, queries=queries, score_grad=score_grad)


def reference(grad_out, slot_weight, slot_pos, slot_rows, values, first_moment, second_moment, row_steps, queries, score_grad):
    positions = jnp.arange(N_TABLE * CAP, dtype=jnp.int32)
    owner_base = (jnp.arange(N_TABLE, dtype=jnp.int32) * R_OWN)[:, None]
    grad_dev = grad_out.reshape(DEVICES, TOK_DEV, D)
    weight_dev = slot_weight.reshape(DEVICES, TOK_DEV, K)
    pos_dev = slot_pos.reshape(DEVICES, TOK_DEV, K)
    query_dev = queries.reshape(DEVICES, TOK_DEV, 2, KD)
    score_dev = score_grad.reshape(DEVICES, TOK_DEV, 2, NSUB)

    def one_device(carry, inputs):
        row_grad, sub_total = carry
        grads, weights, poss, quers, scores, source = inputs
        hits = poss[:, :, None] == positions[None, None, :]
        slot_mix = lax.optimization_barrier(jnp.sum(jnp.where(hits, weights[:, :, None], jnp.float32(0.0)), axis=1)).astype(jnp.bfloat16)
        combined = jnp.dot(slot_mix.T, grads, preferred_element_type=jnp.float32).astype(jnp.bfloat16)
        targets = (owner_base + lax.dynamic_index_in_dim(slot_rows, source, 1, keepdims=False)).reshape(-1)
        row_grad = row_grad.at[targets].add(combined.astype(jnp.float32))
        sub_total = sub_total + jnp.einsum('ths,thk->hsk', scores.astype(jnp.float32), quers.astype(jnp.float32))
        return ((row_grad, sub_total), None)
    start = (jnp.zeros((TOUCHED, D), jnp.float32), jnp.zeros((2, NSUB, KD), jnp.float32))
    sources = jnp.arange(DEVICES, dtype=jnp.int32)
    (row_grad, sub_total), _ = lax.scan(one_device, start, (grad_dev, weight_dev, pos_dev, query_dev, score_dev, sources))
    new_first = 0.9 * first_moment + 0.1 * row_grad
    new_second = 0.95 * second_moment + 0.05 * row_grad * row_grad
    steps = row_steps.astype(jnp.float32)[:, None]
    fix_first = 1.0 - jnp.exp(steps * jnp.log(jnp.float32(0.9)))
    fix_second = 1.0 - jnp.exp(steps * jnp.log(jnp.float32(0.95)))
    new_values = values - 0.1 * (new_first / fix_first) / (jnp.sqrt(new_second / fix_second) + 1e-08)
    return (new_values, new_first, new_second, sub_total.astype(jnp.bfloat16))
```

```python
import jax
import jax.numpy as jnp
from jax import lax
from jax.experimental import pallas as pl
from jax.experimental.pallas import tpu as pltpu
from jax.sharding import PartitionSpec as P

AXES = ("dp", "table")
ROLES = (("x", "y", "z"), ("z", "x", "y"))
BF = jnp.bfloat16
F32 = jnp.float32


def coords(i):
    dp, table = i // 16, i % 16
    return {"x": dp // 2, "core": dp % 2, "y": table // 4, "z": table % 4}


def index_of(c):
    return (c["x"] * 2 + c["core"]) * 16 + c["y"] * 4 + c["z"]


def ring(role, shift):
    pairs = []
    for i in range(128):
        c = coords(i)
        axis = ROLES[c["core"]][role]
        c[axis] = (c[axis] + shift) % 4
        pairs.append((i, index_of(c)))
    return pairs


SWAP = [(i, i ^ 16) for i in range(128)]


def send(value, pairs):
    return lax.ppermute(value, AXES, pairs)


def combine_kernel(pos_ref, weight_ref, grad_ref, out_ref, mix_ref):
    slots, tokens = pos_ref.shape
    rows = mix_ref.shape[0]
    step = 64

    @pl.when(pl.program_id(0) == 0)
    def _():
        def block(b, carry):
            base = pl.multiple_of(b * step, step)
            place = lax.broadcasted_iota(jnp.int32, (step, tokens), 0) + base
            total = jnp.zeros((step, tokens), F32)
            for j in range(slots):
                hit = pos_ref[j : j + 1, :] == place
                total = total + jnp.where(hit, weight_ref[j : j + 1, :], 0.0)
            mix_ref[pl.ds(base, step), :] = total.astype(BF)
            return carry

        lax.fori_loop(0, rows // step, block, 0)

    product = jnp.dot(mix_ref[...], grad_ref[...], preferred_element_type=F32)
    out_ref[...] = product.astype(BF).reshape(out_ref.shape)


def combine(slot_pos, slot_weight, grad_out, n_data, n_table, cap):
    tokens, width = grad_out.shape
    slots = slot_pos.shape[1]
    columns = width // n_data
    return pl.pallas_call(
        combine_kernel,
        grid=(n_data,),
        in_specs=[
            pl.BlockSpec((slots, tokens), lambda i: (0, 0)),
            pl.BlockSpec((slots, tokens), lambda i: (0, 0)),
            pl.BlockSpec((tokens, columns), lambda i: (0, i)),
        ],
        out_specs=pl.BlockSpec((n_table, cap, columns), lambda i: (i, 0, 0)),
        out_shape=jax.ShapeDtypeStruct((n_data * n_table, cap, columns), BF),
        scratch_shapes=[pltpu.VMEM((n_table * cap, tokens), BF)],
        compiler_params=pltpu.CompilerParams(vmem_limit_bytes=32 << 20),
        name="combine",
    )(slot_pos.T, slot_weight.T, grad_out)


def partials_kernel(place_ref, score_ref, query_ref, own_ref, other_ref):
    score = score_ref[...].reshape(-1, score_ref.shape[2])
    query = query_ref[...].reshape(-1, query_ref.shape[2]).astype(F32)
    parity = lax.broadcasted_iota(jnp.int32, query.shape, 0) & 1
    own = jnp.where(parity == place_ref[0], query, 0.0)
    both = jnp.concatenate([own, query - own], axis=1).astype(BF)
    product = lax.dot_general(
        score, both, (((0,), (0,)), ((), ())), preferred_element_type=F32
    ).astype(BF)
    for j in range(4):
        rows = product[j * 256 : (j + 1) * 256]
        own_ref[0, (j - place_ref[2] + 4) % 4] = rows[:, :256]
        other_ref[0, (j - place_ref[5] + 4) % 4] = rows[:, 256:]


def partials(places, score, query):
    tokens, halves, keys = score.shape
    depth = query.shape[2]
    shape = jax.ShapeDtypeStruct((4, 4, 256, depth), BF)
    return pl.pallas_call(
        partials_kernel,
        grid_spec=pltpu.PrefetchScalarGridSpec(
            num_scalar_prefetch=1,
            grid=(4,),
            in_specs=[
                pl.BlockSpec((tokens, halves, keys // 4), lambda i, p: (0, 0, i)),
                pl.BlockSpec((tokens, halves, depth), lambda i, p: (0, 0, 0)),
            ],
            out_specs=[
                pl.BlockSpec((1, 4, 256, depth), lambda i, p: ((i - p[1] + 4) % 4, 0, 0, 0)),
                pl.BlockSpec((1, 4, 256, depth), lambda i, p: ((i - p[4] + 4) % 4, 0, 0, 0)),
            ],
        ),
        out_shape=[shape] * 2,
        compiler_params=pltpu.CompilerParams(vmem_limit_bytes=32 << 20),
        name="partials",
    )(places, score, query)


def merge_kernel(own_ref, got_ref, *out_refs):
    for r, out_ref in enumerate(out_refs):
        out_ref[...] = (own_ref[r].astype(F32) + got_ref[r].astype(F32)).astype(BF)


def merge(own, got):
    return pl.pallas_call(
        merge_kernel,
        out_shape=[jax.ShapeDtypeStruct(own.shape[1:], BF)] * 4,
        compiler_params=pltpu.CompilerParams(vmem_limit_bytes=32 << 20),
        name="merge",
    )(own, got)


def sum_kernel(a_ref, b_ref, c_ref, d_ref, *out_refs):
    for r, out_ref in enumerate(out_refs):
        near = a_ref[r].astype(F32) + c_ref[r].astype(F32)
        far = b_ref[r].astype(F32) + d_ref[r].astype(F32)
        out_ref[...] = (near + far).astype(BF)


def sum_chunks(chunks):
    shape = jax.ShapeDtypeStruct(chunks[0].shape[1:], BF)
    return pl.pallas_call(
        sum_kernel,
        out_shape=[shape] * 4,
        compiler_params=pltpu.CompilerParams(vmem_limit_bytes=32 << 20),
        name="sum_chunks",
    )(*chunks)


def place_kernel(place_ref, *refs):
    blocks, (out_ref, held, sem_in, sem_out) = refs[:8], refs[8:]
    loads = [pltpu.make_async_copy(blocks[k], held.at[k], sem_in.at[k]) for k in range(8)]
    for load in loads:
        load.start()
    stores = []
    for k in range(8):
        half, rb = k // 4, k % 4
        loads[k].wait()
        for ra in range(4):
            a = (place_ref[3 * half + 1] + ra) % 4
            b = (place_ref[3 * half + 2] + rb) % 4
            start = pl.multiple_of((a * 4 + b) * 256, 256)
            store = pltpu.make_async_copy(
                held.at[k, ra],
                out_ref.at[place_ref[3 * half], pl.ds(start, 256)],
                sem_out.at[k * 4 + ra],
            )
            store.start()
            stores.append(store)
    for store in stores:
        store.wait()


def place_blocks(places, buffers):
    return pl.pallas_call(
        place_kernel,
        in_specs=[pl.BlockSpec(memory_space=pltpu.SMEM)] + [pl.BlockSpec(memory_space=pl.ANY)] * 8,
        out_specs=pl.BlockSpec(memory_space=pl.ANY),
        out_shape=jax.ShapeDtypeStruct((2, 4096, 256), BF),
        scratch_shapes=[
            pltpu.VMEM((8, *buffers[0].shape), BF),
            pltpu.SemaphoreType.DMA((8,)),
            pltpu.SemaphoreType.DMA((32,)),
        ],
        compiler_params=pltpu.CompilerParams(vmem_limit_bytes=16 << 20),
        name="place_blocks",
    )(places, *buffers)


def adam_kernel(index_ref, steps_ref, arrived_ref, v_ref, m_ref, s_ref, nv_ref, nm_ref, ns_ref):
    rows, columns = v_ref.shape
    slots = index_ref.shape[1]
    base = pl.program_id(0) * rows
    place = lax.broadcasted_iota(jnp.int32, (rows, slots), 0) + base
    selector = jnp.where(index_ref[...] == place, 1.0, 0.0).astype(BF)
    grad = jnp.dot(selector, arrived_ref[...], preferred_element_type=F32)
    steps = steps_ref[0].astype(F32)
    first = 1.0 / (1.0 - jnp.exp(steps * jnp.log(jnp.float32(0.9))))
    second = 1.0 / (1.0 - jnp.exp(steps * jnp.log(jnp.float32(0.95))))
    first = jnp.broadcast_to(first, (128, rows)).T[:, :1]
    second = jnp.broadcast_to(second, (128, rows)).T[:, :1]
    new_first = 0.9 * m_ref[...] + 0.1 * grad
    new_second = 0.95 * s_ref[...] + 0.05 * grad * grad
    nm_ref[...] = new_first
    ns_ref[...] = new_second
    nv_ref[...] = v_ref[...] - 0.1 * (new_first * first) / (jnp.sqrt(new_second * second) + 1e-08)


def adam(index, steps, arrived, values, first_moment, second_moment):
    owned, columns = values.shape
    rows = 256
    slots = index.shape[1]
    block = pl.BlockSpec((rows, columns), lambda i: (i, 0))
    shape = jax.ShapeDtypeStruct(values.shape, F32)
    return pl.pallas_call(
        adam_kernel,
        grid=(owned // rows,),
        in_specs=[
            pl.BlockSpec((1, slots), lambda i: (0, 0)),
            pl.BlockSpec((1, 1, rows), lambda i: (i, 0, 0)),
            pl.BlockSpec((slots, columns), lambda i: (0, 0)),
            block,
            block,
            block,
        ],
        out_specs=[block] * 3,
        out_shape=[shape] * 3,
        compiler_params=pltpu.CompilerParams(vmem_limit_bytes=40 << 20),
        name="adam",
    )(index, steps, arrived, values, first_moment, second_moment)


def places_of():
    dp, table = lax.axis_index("dp"), lax.axis_index("table")
    at = {"x": dp // 2, "y": table // 4, "z": table % 4}
    core = dp % 2
    rows = []
    for c in (core, 1 - core):
        a = jnp.where(c == 0, at[ROLES[0][0]], at[ROLES[1][0]])
        b = jnp.where(c == 0, at[ROLES[0][1]], at[ROLES[1][1]])
        rows += [c, a, b]
    return jnp.stack(rows).astype(jnp.int32)


def per_device(
    grad_out,
    slot_weight,
    slot_pos,
    slot_rows,
    values,
    first_moment,
    second_moment,
    row_steps,
    queries,
    score_grad,
):
    n_table = lax.axis_size("table")
    n_data = lax.axis_size("dp")
    cap = slot_rows.shape[2]
    columns = values.shape[1]
    places = places_of()

    own, other = partials(places, score_grad, queries)
    got = send(other, SWAP)
    ordered = combine(slot_pos, slot_weight, grad_out, n_data, n_table, cap)
    chunks = merge(own, got)
    ordered, chunks = lax.optimization_barrier((ordered, chunks))
    chunks = [chunks[0]] + [send(chunks[r], ring(0, r)) for r in (1, 2, 3)]
    arrived = lax.all_to_all(ordered, AXES, split_axis=0, concat_axis=0, tiled=True)
    parts = sum_chunks(chunks)
    parts = [parts[0]] + [send(parts[r], ring(1, r)) for r in (1, 2, 3)]
    near = parts[0].astype(F32) + parts[2].astype(F32)
    total = (near + (parts[1].astype(F32) + parts[3].astype(F32))).astype(BF)
    around = [send(total, ring(2, r)) for r in (1, 2, 3)]
    near = total.astype(F32) + around[1].astype(F32)
    final = (near + (around[0].astype(F32) + around[2].astype(F32))).astype(BF)
    mine = jnp.stack([final] + [send(final, ring(0, -r)) for r in (1, 2, 3)])
    buffers = [mine] + [send(mine, ring(1, -r)) for r in (1, 2, 3)]
    buffers += [send(b, SWAP) for b in buffers]
    outs = adam(
        slot_rows.reshape(1, -1),
        row_steps.reshape(-1, 1, 256),
        arrived.reshape(-1, columns),
        values,
        first_moment,
        second_moment,
    )
    places, outs = lax.optimization_barrier((places, outs))
    subkey_out = place_blocks(places, buffers)
    return (*outs, subkey_out)


def solution(mesh):
    return jax.shard_map(
        per_device,
        mesh=mesh,
        in_specs=(
            P(("dp", "table"), None),
            P(("dp", "table"), None),
            P(("dp", "table"), None),
            P("table", None, None),
            P("table", "dp"),
            P("table", "dp"),
            P("table", "dp"),
            P("table"),
            P(("dp", "table"), None, None),
            P(("dp", "table"), None, None),
        ),
        out_specs=(P("table", "dp"), P("table", "dp"), P("table", "dp"), P()),
        check_vma=False,
    )
```

```python
import jax
import jax.numpy as jnp
from jax import lax
from jax.experimental import pallas as pl
from jax.experimental.pallas import tpu as pltpu
from jax.sharding import PartitionSpec as P

AXES = ("dp", "table")
ROLES = (("x", "y", "z"), ("z", "x", "y"))
BF = jnp.bfloat16
F32 = jnp.float32


def coords(i):
    dp, table = i // 16, i % 16
    return {"x": dp // 2, "core": dp % 2, "y": table // 4, "z": table % 4}


def index_of(c):
    return (c["x"] * 2 + c["core"]) * 16 + c["y"] * 4 + c["z"]


def ring(role, shift):
    pairs = []
    for i in range(128):
        c = coords(i)
        axis = ROLES[c["core"]][role]
        c[axis] = (c[axis] + shift) % 4
        pairs.append((i, index_of(c)))
    return pairs


SWAP = [(i, i ^ 16) for i in range(128)]


def send(value, pairs):
    return lax.ppermute(value, AXES, pairs)


def in_hbm(value):
    return pltpu.with_memory_space_constraint(value, pltpu.HBM)


BESIDE_TRANSFER = pl.CostEstimate(flops=10**11, bytes_accessed=0, transcendentals=0)


def first_kernel(pos_ref, weight_ref, grad_ref, out_ref, mix_ref):
    slots, tokens = pos_ref.shape
    rows = mix_ref.shape[0]
    step = 64

    @pl.when(pl.program_id(0) == 0)
    def _():
        def block(b, carry):
            base = pl.multiple_of(b * step, step)
            place = lax.broadcasted_iota(jnp.int32, (step, tokens), 0) + base
            total = jnp.zeros((step, tokens), F32)
            for j in range(slots):
                hit = pos_ref[j : j + 1, :] == place
                total = total + jnp.where(hit, weight_ref[j : j + 1, :], 0.0)
            mix_ref[pl.ds(base, step), :] = total.astype(BF)
            return carry

        lax.fori_loop(0, rows // step, block, 0)

    product = jnp.dot(mix_ref[...], grad_ref[...], preferred_element_type=F32)
    out_ref[...] = product.astype(BF).reshape(out_ref.shape)


def next_kernel(mix_ref, grad_ref, out_ref):
    product = jnp.dot(mix_ref[...], grad_ref[...], preferred_element_type=F32)
    out_ref[...] = product.astype(BF).reshape(out_ref.shape)


def combine(slot_pos, slot_weight, grad_out, n_data, n_table, cap, pieces):
    tokens, width = grad_out.shape
    rows = n_table * cap
    columns = width // n_data // pieces
    slots = pl.BlockSpec((slot_pos.shape[1], tokens), lambda i: (0, 0))
    mixed = pl.BlockSpec((rows, tokens), lambda i: (0, 0))
    out_spec = pl.BlockSpec((n_table, cap, columns), lambda i: (i, 0, 0))
    out_shape = pltpu.HBM((n_data * n_table, cap, columns), BF)
    params = pltpu.CompilerParams(vmem_limit_bytes=32 << 20)

    def grad(k):
        return pl.BlockSpec((tokens, columns), lambda i: (0, i * pieces + k))

    first, mix = pl.pallas_call(
        first_kernel,
        grid=(n_data,),
        in_specs=[slots, slots, grad(0)],
        out_specs=[out_spec, mixed],
        out_shape=[out_shape, pltpu.HBM((rows, tokens), BF)],
        compiler_params=params,
        name="combine_first",
    )(slot_pos.T, slot_weight.T, grad_out)
    rest = [
        pl.pallas_call(
            next_kernel,
            grid=(n_data,),
            in_specs=[mixed, grad(k)],
            out_specs=out_spec,
            out_shape=out_shape,
            compiler_params=params,
            name="combine_next",
        )(mix, grad_out)
        for k in range(1, pieces)
    ]
    return [first, *rest]


def partials_kernel(place_ref, score_ref, query_ref, own_ref, other_ref):
    score = score_ref[...].reshape(-1, score_ref.shape[2])
    query = query_ref[...].reshape(-1, query_ref.shape[2]).astype(F32)
    parity = lax.broadcasted_iota(jnp.int32, query.shape, 0) & 1
    own = jnp.where(parity == place_ref[0], query, 0.0)
    both = jnp.concatenate([own, query - own], axis=1).astype(BF)
    product = lax.dot_general(
        score, both, (((0,), (0,)), ((), ())), preferred_element_type=F32
    ).astype(BF)
    for j in range(4):
        rows = product[j * 256 : (j + 1) * 256]
        own_ref[0, (j - place_ref[2] + 4) % 4] = rows[:, :256]
        other_ref[0, (j - place_ref[5] + 4) % 4] = rows[:, 256:]


def partials(places, score, query):
    tokens, halves, keys = score.shape
    depth = query.shape[2]
    shape = jax.ShapeDtypeStruct((4, 4, 256, depth), BF)
    return pl.pallas_call(
        partials_kernel,
        grid_spec=pltpu.PrefetchScalarGridSpec(
            num_scalar_prefetch=1,
            grid=(4,),
            in_specs=[
                pl.BlockSpec((tokens, halves, keys // 4), lambda i, p: (0, 0, i)),
                pl.BlockSpec((tokens, halves, depth), lambda i, p: (0, 0, 0)),
            ],
            out_specs=[
                pl.BlockSpec((1, 4, 256, depth), lambda i, p: ((i - p[1] + 4) % 4, 0, 0, 0)),
                pl.BlockSpec((1, 4, 256, depth), lambda i, p: ((i - p[4] + 4) % 4, 0, 0, 0)),
            ],
        ),
        out_shape=[shape] * 2,
        compiler_params=pltpu.CompilerParams(vmem_limit_bytes=32 << 20),
        name="partials",
    )(places, score, in_hbm(query))


def merge_kernel(own_ref, got_ref, *out_refs):
    for r, out_ref in enumerate(out_refs):
        out_ref[...] = (own_ref[r].astype(F32) + got_ref[r].astype(F32)).astype(BF)


def merge(own, got):
    return pl.pallas_call(
        merge_kernel,
        out_shape=[jax.ShapeDtypeStruct(own.shape[1:], BF)] * 4,
        compiler_params=pltpu.CompilerParams(vmem_limit_bytes=32 << 20),
        name="merge",
    )(own, got)


def sum_kernel(a_ref, b_ref, c_ref, d_ref, *out_refs):
    for r, out_ref in enumerate(out_refs):
        near = a_ref[r].astype(F32) + c_ref[r].astype(F32)
        far = b_ref[r].astype(F32) + d_ref[r].astype(F32)
        out_ref[...] = (near + far).astype(BF)


def sum_chunks(chunks, cost=None):
    shape = pltpu.HBM(chunks[0].shape[1:], BF)
    return pl.pallas_call(
        sum_kernel,
        out_shape=[shape] * 4,
        cost_estimate=cost,
        compiler_params=pltpu.CompilerParams(vmem_limit_bytes=32 << 20),
        name="sum_chunks",
    )(*chunks)


def sum_all_kernel(a_ref, b_ref, c_ref, d_ref, out_ref):
    near = a_ref[...].astype(F32) + c_ref[...].astype(F32)
    far = b_ref[...].astype(F32) + d_ref[...].astype(F32)
    out_ref[...] = (near + far).astype(BF)


def sum_all(chunks, cost=None):
    return pl.pallas_call(
        sum_all_kernel,
        out_shape=jax.ShapeDtypeStruct(chunks[0].shape, BF),
        cost_estimate=cost,
        name="sum_all",
    )(*chunks)


def place_kernel(place_ref, *refs):
    blocks = refs[:4]
    out_ref, held, sem_in, sem_out = refs[-4:]
    loads = [pltpu.make_async_copy(blocks[k], held.at[k], sem_in.at[k]) for k in range(4)]
    for load in loads:
        load.start()
    stores = []
    for rb in range(4):
        loads[rb].wait()
        for ra in range(4):
            a = (place_ref[1] + ra) % 4
            b = (place_ref[2] + rb) % 4
            start = pl.multiple_of((a * 4 + b) * 256, 256)
            store = pltpu.make_async_copy(
                held.at[rb, ra],
                out_ref.at[place_ref[0], pl.ds(start, 256)],
                sem_out.at[rb * 4 + ra],
            )
            store.start()
            stores.append(store)
    for store in stores:
        store.wait()


def place_half(place, buffers, out=()):
    return pl.pallas_call(
        place_kernel,
        in_specs=[pl.BlockSpec(memory_space=pltpu.SMEM)]
        + [pl.BlockSpec(memory_space=pl.ANY)] * (4 + len(out)),
        out_specs=pl.BlockSpec(memory_space=pl.ANY),
        out_shape=jax.ShapeDtypeStruct((2, 4096, 256), BF),
        input_output_aliases={5: 0} if out else {},
        scratch_shapes=[
            pltpu.VMEM((4, *buffers[0].shape), BF),
            pltpu.SemaphoreType.DMA((4,)),
            pltpu.SemaphoreType.DMA((16,)),
        ],
        compiler_params=pltpu.CompilerParams(vmem_limit_bytes=16 << 20),
        name="place_half",
    )(place, *buffers, *out)


def adam_kernel(index_ref, steps_ref, *refs):
    rows = steps_ref.shape[2]
    slots = index_ref.shape[1]
    v_ref, m_ref, s_ref = refs[-6:-3] if len(refs) < 9 else refs[-9:-6]
    nv_ref, nm_ref, ns_ref = refs[-3:]
    arrived = refs[: len(refs) - (6 if len(refs) < 9 else 9)]
    base = pl.program_id(0) * rows
    place = lax.broadcasted_iota(jnp.int32, (rows, slots), 0) + base
    selector = jnp.where(index_ref[...] == place, 1.0, 0.0).astype(BF)
    grad = [jnp.dot(selector, a[...], preferred_element_type=F32) for a in arrived]
    grad = grad[0] if len(grad) == 1 else jnp.concatenate(grad, axis=1)
    steps = steps_ref[0].astype(F32)
    first = 1.0 / (1.0 - jnp.exp(steps * jnp.log(jnp.float32(0.9))))
    second = 1.0 / (1.0 - jnp.exp(steps * jnp.log(jnp.float32(0.95))))
    first = jnp.broadcast_to(first, (128, rows)).T[:, :1]
    second = jnp.broadcast_to(second, (128, rows)).T[:, :1]
    new_first = 0.9 * m_ref[...] + 0.1 * grad
    new_second = 0.95 * s_ref[...] + 0.05 * grad * grad
    nm_ref[...] = new_first
    ns_ref[...] = new_second
    nv_ref[...] = v_ref[...] - 0.1 * (new_first * first) / (jnp.sqrt(new_second * second) + 1e-08)


def adam(index, steps, arrived, state, column, done=(), cost=None):
    owned = state[0].shape[0]
    rows = steps.shape[2]
    slots = index.shape[1]
    width = sum(a.shape[1] for a in arrived)
    block = pl.BlockSpec((rows, width), lambda i: (i, column))
    shape = jax.ShapeDtypeStruct(state[0].shape, F32)
    before = 2 + len(arrived) + 3
    return pl.pallas_call(
        adam_kernel,
        grid=(owned // rows,),
        in_specs=[
            pl.BlockSpec((1, slots), lambda i: (0, 0)),
            pl.BlockSpec((1, 1, rows), lambda i: (i, 0, 0)),
        ]
        + [pl.BlockSpec(a.shape, lambda i: (0, 0)) for a in arrived]
        + [block] * 3
        + [pl.BlockSpec(memory_space=pl.ANY)] * len(done),
        out_specs=[block] * 3,
        out_shape=[shape] * 3,
        input_output_aliases={before + k: k for k in range(len(done))},
        cost_estimate=cost,
        compiler_params=pltpu.CompilerParams(vmem_limit_bytes=40 << 20),
        name="adam",
    )(index, steps, *arrived, *[in_hbm(x) for x in state], *done)


def stack_kernel(*refs):
    for k, ref in enumerate(refs[:-1]):
        refs[-1][k] = ref[...]


def stack(blocks, cost=None):
    return pl.pallas_call(
        stack_kernel,
        out_shape=pltpu.HBM((len(blocks), *blocks[0].shape), BF),
        cost_estimate=cost,
        name="stack",
    )(*blocks)


def places_of():
    dp, table = lax.axis_index("dp"), lax.axis_index("table")
    at = {"x": dp // 2, "y": table // 4, "z": table % 4}
    core = dp % 2
    rows = []
    for c in (core, 1 - core):
        a = jnp.where(c == 0, at[ROLES[0][0]], at[ROLES[1][0]])
        b = jnp.where(c == 0, at[ROLES[0][1]], at[ROLES[1][1]])
        rows += [c, a, b]
    return jnp.stack(rows).astype(jnp.int32)


def per_device(
    grad_out,
    slot_weight,
    slot_pos,
    slot_rows,
    values,
    first_moment,
    second_moment,
    row_steps,
    queries,
    score_grad,
):
    n_table = lax.axis_size("table")
    n_data = lax.axis_size("dp")
    cap = slot_rows.shape[2]
    places = places_of()

    def exchange(ordered):
        moved = lax.all_to_all(ordered, AXES, split_axis=0, concat_axis=0, tiled=True)
        return moved.reshape(-1, moved.shape[2])

    own, other = partials(places, score_grad, queries)
    got = send(other, SWAP)
    ordered = combine(slot_pos, slot_weight, grad_out, n_data, n_table, cap, 2)
    chunks = merge(own, got)
    ordered[0], chunks = lax.optimization_barrier((ordered[0], chunks))
    chunks = [chunks[0]] + [send(chunks[r], ring(0, r)) for r in (1, 2, 3)]
    arrived = [exchange(ordered[0])]
    parts = sum_chunks(chunks, BESIDE_TRANSFER)
    parts = [parts[0]] + [send(parts[r], ring(1, r)) for r in (1, 2, 3)]
    total = sum_all(parts)
    ordered[1], total = lax.optimization_barrier((ordered[1], total))
    around = [total] + [send(total, ring(2, r)) for r in (1, 2, 3)]
    arrived.append(exchange(ordered[1]))
    final = sum_all(around, BESIDE_TRANSFER)
    mine = [final] + [send(final, ring(0, -r)) for r in (1, 2, 3)]

    index = slot_rows.reshape(1, -1)
    steps = row_steps.reshape(-1, 1, 256)
    state = (values, first_moment, second_moment)
    outs = adam(index, steps, arrived[:1], state, 0)
    mine, outs = lax.optimization_barrier((mine, outs))
    mine = jnp.stack(mine)
    buffers = [mine] + [send(mine, ring(1, -r)) for r in (1, 2, 3)]
    outs = adam(index, steps, arrived[1:], state, 1, outs)
    buffers[1:], outs = lax.optimization_barrier((buffers[1:], outs))
    theirs = [send(b, SWAP) for b in buffers]
    subkey_out = place_half(places[:3], buffers)
    subkey_out = place_half(places[3:], theirs, (subkey_out,))
    return (*outs, subkey_out)


def solution(mesh):
    return jax.shard_map(
        per_device,
        mesh=mesh,
        in_specs=(
            P(("dp", "table"), None),
            P(("dp", "table"), None),
            P(("dp", "table"), None),
            P("table", None, None),
            P("table", "dp"),
            P("table", "dp"),
            P("table", "dp"),
            P("table"),
            P(("dp", "table"), None, None),
            P(("dp", "table"), None, None),
        ),
        out_specs=(P("table", "dp"), P("table", "dp"), P("table", "dp"), P()),
        check_vma=False,
    )
```

```python
import jax
import jax.numpy as jnp
from jax import lax
from jax.experimental import pallas as pl
from jax.experimental.pallas import tpu as pltpu
from jax.sharding import PartitionSpec as P

AXES = ("dp", "table")
ROLES = (("x", "y", "z"), ("y", "z", "x"))
BF = jnp.bfloat16
F32 = jnp.float32


def coords(i):
    dp, table = i // 16, i % 16
    return {"x": dp // 2, "core": dp % 2, "y": table // 4, "z": table % 4}


def index_of(c):
    return (c["x"] * 2 + c["core"]) * 16 + c["y"] * 4 + c["z"]


def ring(role, shift):
    pairs = []
    for i in range(128):
        c = coords(i)
        axis = ROLES[c["core"]][role]
        c[axis] = (c[axis] + shift) % 4
        pairs.append((i, index_of(c)))
    return pairs


SWAP = [(i, i ^ 16) for i in range(128)]


def send(value, pairs):
    return lax.ppermute(value, AXES, pairs)


def in_hbm(value):
    return pltpu.with_memory_space_constraint(value, pltpu.HBM)


BESIDE_TRANSFER = pl.CostEstimate(flops=10**11, bytes_accessed=0, transcendentals=0)


def first_kernel(pos_ref, weight_ref, low_ref, high_ref, out_ref, mix_ref):
    slots, tokens = pos_ref.shape
    rows = mix_ref.shape[0]
    step = 64

    @pl.when(pl.program_id(0) == 0)
    def _():
        def block(b, carry):
            base = pl.multiple_of(b * step, step)
            place = lax.broadcasted_iota(jnp.int32, (step, tokens), 0) + base
            total = jnp.zeros((step, tokens), F32)
            for j in range(slots):
                hit = pos_ref[j : j + 1, :] == place
                total = total + jnp.where(hit, weight_ref[j : j + 1, :], 0.0)
            mix_ref[pl.ds(base, step), :] = total.astype(BF)
            return carry

        lax.fori_loop(0, rows // step, block, 0)

    next_kernel(None, mix_ref, low_ref, high_ref, out_ref)


def next_kernel(after_ref, mix_ref, low_ref, high_ref, out_ref):
    half = out_ref.shape[0] // 2
    for k, grad_ref in enumerate((low_ref, high_ref)):
        product = jnp.dot(mix_ref[...], grad_ref[...], preferred_element_type=F32)
        out_ref[k * half : (k + 1) * half] = product.astype(BF).reshape(half, *out_ref.shape[1:])


def combine(after, slot_pos, slot_weight, grad_out, mix, n_data, n_table, cap, start, w):
    tokens, width = grad_out.shape
    rows = n_table * cap
    blocks = width // n_data // w
    slots = pl.BlockSpec((slot_pos.shape[1], tokens), lambda i: (0, 0))
    mixed = pl.BlockSpec((rows, tokens), lambda i: (0, 0))
    grads = [
        pl.BlockSpec((tokens, w), lambda i, half=half: (0, (2 * i + half) * blocks + start // w))
        for half in range(2)
    ]
    out_spec = pl.BlockSpec((2 * n_table, cap, w), lambda i: (i, 0, 0))
    out_shape = pltpu.HBM((n_data * n_table, cap, w), BF)
    params = pltpu.CompilerParams(vmem_limit_bytes=32 << 20)
    anywhere = pl.BlockSpec(memory_space=pl.ANY)
    if mix is None:
        return pl.pallas_call(
            first_kernel,
            grid=(n_data // 2,),
            in_specs=[slots, slots, *grads],
            out_specs=[out_spec, mixed],
            out_shape=[out_shape, pltpu.HBM((rows, tokens), BF)],
            compiler_params=params,
            name="combine_first",
        )(slot_pos.T, slot_weight.T, grad_out, grad_out)
    return pl.pallas_call(
        next_kernel,
        grid=(n_data // 2,),
        in_specs=[anywhere, mixed, *grads],
        out_specs=out_spec,
        out_shape=out_shape,
        compiler_params=params,
        name="combine_next",
    )(after, mix, grad_out, grad_out)


def partials_kernel(place_ref, score_ref, query_ref, own_ref, other_ref):
    score = score_ref[...].reshape(-1, score_ref.shape[2])
    query = query_ref[...].reshape(-1, query_ref.shape[2]).astype(F32)
    parity = lax.broadcasted_iota(jnp.int32, query.shape, 0) & 1
    own = jnp.where(parity == place_ref[0], query, 0.0)
    both = jnp.concatenate([own, query - own], axis=1).astype(BF)
    product = lax.dot_general(
        score, both, (((0,), (0,)), ((), ())), preferred_element_type=F32
    ).astype(BF)
    own_ref[0] = product[:, : own_ref.shape[2]]
    other_ref[0] = product[:, own_ref.shape[2] :]


def partials(places, score, query):
    tokens, halves, keys = score.shape
    depth = query.shape[2]
    rows = keys // 4
    shape = jax.ShapeDtypeStruct((4, rows, depth), BF)
    return pl.pallas_call(
        partials_kernel,
        grid_spec=pltpu.PrefetchScalarGridSpec(
            num_scalar_prefetch=1,
            grid=(4,),
            in_specs=[
                pl.BlockSpec((tokens, halves, rows), lambda i, p: (0, 0, i)),
                pl.BlockSpec((tokens, halves, depth), lambda i, p: (0, 0, 0)),
            ],
            out_specs=[
                pl.BlockSpec((1, rows, depth), lambda i, p: ((i - p[1] + 4) % 4, 0, 0)),
                pl.BlockSpec((1, rows, depth), lambda i, p: ((i - p[3] + 4) % 4, 0, 0)),
            ],
        ),
        out_shape=[shape] * 2,
        compiler_params=pltpu.CompilerParams(vmem_limit_bytes=32 << 20),
        name="partials",
    )(places, score, in_hbm(query))


def merge_kernel(own_ref, got_ref, *out_refs):
    for r, out_ref in enumerate(out_refs):
        out_ref[...] = (own_ref[r].astype(F32) + got_ref[r].astype(F32)).astype(BF)


def merge(own, got):
    return pl.pallas_call(
        merge_kernel,
        out_shape=[jax.ShapeDtypeStruct(own.shape[1:], BF)] * 4,
        compiler_params=pltpu.CompilerParams(vmem_limit_bytes=32 << 20),
        name="merge",
    )(own, got)


def sum_kernel(a_ref, b_ref, c_ref, d_ref, out_ref):
    near = a_ref[...].astype(F32) + c_ref[...].astype(F32)
    far = b_ref[...].astype(F32) + d_ref[...].astype(F32)
    out_ref[...] = (near + far).astype(BF)


def sum_chunks(chunks):
    return pl.pallas_call(
        sum_kernel,
        out_shape=pltpu.HBM(chunks[0].shape, BF),
        cost_estimate=BESIDE_TRANSFER,
        compiler_params=pltpu.CompilerParams(vmem_limit_bytes=32 << 20),
        name="sum_chunks",
    )(*chunks)


def add_four(chunks):
    near = chunks[0].astype(F32) + chunks[2].astype(F32)
    return (near + (chunks[1].astype(F32) + chunks[3].astype(F32))).astype(BF)


def place_kernel(place_ref, *refs):
    blocks = refs[:4]
    out_ref, held, sem_in, sem_out = refs[-4:]
    rows = held.shape[1]
    loads = [pltpu.make_async_copy(blocks[k], held.at[k], sem_in.at[k]) for k in range(4)]
    for load in loads:
        load.start()
    stores = []
    for k in range(4):
        loads[k].wait()
        start = pl.multiple_of((place_ref[1] + k) % 4 * rows, rows)
        store = pltpu.make_async_copy(
            held.at[k], out_ref.at[place_ref[0], pl.ds(start, rows)], sem_out.at[k]
        )
        store.start()
        stores.append(store)
    for store in stores:
        store.wait()


def place_half(place, buffers, out=()):
    return pl.pallas_call(
        place_kernel,
        in_specs=[pl.BlockSpec(memory_space=pltpu.SMEM)]
        + [pl.BlockSpec(memory_space=pl.ANY)] * (4 + len(out)),
        out_specs=pl.BlockSpec(memory_space=pl.ANY),
        out_shape=jax.ShapeDtypeStruct((2, 4096, 256), BF),
        input_output_aliases={5: 0} if out else {},
        scratch_shapes=[
            pltpu.VMEM((4, *buffers[0].shape), BF),
            pltpu.SemaphoreType.DMA((4,)),
            pltpu.SemaphoreType.DMA((4,)),
        ],
        compiler_params=pltpu.CompilerParams(vmem_limit_bytes=16 << 20),
        name="place_half",
    )(place, *buffers, *out)


def adam_kernel(index_ref, steps_ref, *refs):
    rows = steps_ref.shape[2]
    slots = index_ref.shape[1]
    v_ref, m_ref, s_ref = refs[-6:-3] if len(refs) < 9 else refs[-9:-6]
    nv_ref, nm_ref, ns_ref = refs[-3:]
    arrived = refs[: len(refs) - (6 if len(refs) < 9 else 9)]
    base = pl.program_id(0) * rows
    place = lax.broadcasted_iota(jnp.int32, (rows, slots), 0) + base
    selector = jnp.where(index_ref[...] == place, 1.0, 0.0).astype(BF)
    grad = [jnp.dot(selector, a[...], preferred_element_type=F32) for a in arrived]
    grad = grad[0] if len(grad) == 1 else jnp.concatenate(grad, axis=1)
    steps = steps_ref[0].astype(F32)
    first = 1.0 / (1.0 - jnp.exp(steps * jnp.log(jnp.float32(0.9))))
    second = 1.0 / (1.0 - jnp.exp(steps * jnp.log(jnp.float32(0.95))))
    first = jnp.broadcast_to(first, (128, rows)).T[:, :1]
    second = jnp.broadcast_to(second, (128, rows)).T[:, :1]
    new_first = 0.9 * m_ref[...] + 0.1 * grad
    new_second = 0.95 * s_ref[...] + 0.05 * grad * grad
    nm_ref[...] = new_first
    ns_ref[...] = new_second
    nv_ref[...] = v_ref[...] - 0.1 * (new_first * first) / (jnp.sqrt(new_second * second) + 1e-08)


def adam(index, steps, arrived, state, column, done=(), cost=None):
    owned = state[0].shape[0]
    rows = steps.shape[2]
    slots = index.shape[1]
    width = sum(a.shape[1] for a in arrived)
    block = pl.BlockSpec((rows, width), lambda i: (i, column))
    shape = jax.ShapeDtypeStruct(state[0].shape, F32)
    before = 2 + len(arrived) + 3
    return pl.pallas_call(
        adam_kernel,
        grid=(owned // rows,),
        in_specs=[
            pl.BlockSpec((1, slots), lambda i: (0, 0)),
            pl.BlockSpec((1, 1, rows), lambda i: (i, 0, 0)),
        ]
        + [pl.BlockSpec(a.shape, lambda i: (0, 0)) for a in arrived]
        + [block] * 3
        + [pl.BlockSpec(memory_space=pl.ANY)] * len(done),
        out_specs=[block] * 3,
        out_shape=[shape] * 3,
        input_output_aliases={before + k: k for k in range(len(done))},
        cost_estimate=cost,
        compiler_params=pltpu.CompilerParams(vmem_limit_bytes=40 << 20),
        name="adam",
    )(index, steps, *arrived, *[in_hbm(x) for x in state], *done)


def stack_kernel(*refs):
    for k, ref in enumerate(refs[:-1]):
        refs[-1][k] = ref[...]


def stack(blocks, cost=None):
    return pl.pallas_call(
        stack_kernel,
        out_shape=pltpu.HBM((len(blocks), *blocks[0].shape), BF),
        cost_estimate=cost,
        name="stack",
    )(*blocks)


def places_of():
    dp, table = lax.axis_index("dp"), lax.axis_index("table")
    at = {"x": dp // 2, "y": table // 4, "z": table % 4}
    core = dp % 2
    rows = []
    for c in (core, 1 - core):
        rows += [c, jnp.where(c == 0, at[ROLES[0][0]], at[ROLES[1][0]])]
    return jnp.stack(rows).astype(jnp.int32)


def per_device(
    grad_out,
    slot_weight,
    slot_pos,
    slot_rows,
    values,
    first_moment,
    second_moment,
    row_steps,
    queries,
    score_grad,
):
    n_table = lax.axis_size("table")
    n_data = lax.axis_size("dp")
    cap = slot_rows.shape[2]
    places = places_of()

    def exchange(ordered):
        moved = lax.all_to_all(ordered, AXES, split_axis=0, concat_axis=0, tiled=True)
        return moved.reshape(-1, moved.shape[2])

    own, other = partials(places, score_grad, queries)
    got = send(other, SWAP)
    sizes = (n_data, n_table, cap)
    ordered, mix = combine(None, slot_pos, slot_weight, grad_out, None, *sizes, 0, 256)
    chunks = merge(own, got)
    ordered, chunks = lax.optimization_barrier((ordered, chunks))
    chunks = [chunks[0]] + [send(chunks[r], ring(0, r)) for r in (1, 2, 3)]
    arrived = [exchange(ordered)]
    total = sum_chunks(chunks)
    total = add_four([total] + [send(total, ring(1, r)) for r in (1, 2, 3)])
    ordered = combine(total, slot_pos, slot_weight, grad_out, mix, *sizes, 256, 256)
    around = [total] + [send(total, ring(2, r)) for r in (1, 2, 3)]
    arrived.append(exchange(ordered))

    index = slot_rows.reshape(1, -1)
    steps = row_steps.reshape(-1, 1, 256)
    state = (values, first_moment, second_moment)
    outs = adam(index, steps, arrived[:1], state, 0)
    around, outs = lax.optimization_barrier((around, outs))
    final = sum_chunks(around)
    buffers = [final] + [send(final, ring(0, -r)) for r in (1, 2, 3)]
    outs = adam(index, steps, arrived[1:], state, 1, outs)
    buffers[1:], outs = lax.optimization_barrier((buffers[1:], outs))
    theirs = [send(b, SWAP) for b in buffers]
    subkey_out = place_half(places[:2], buffers)
    subkey_out = place_half(places[2:], theirs, (subkey_out,))
    return (*outs, subkey_out)


def solution(mesh):
    return jax.shard_map(
        per_device,
        mesh=mesh,
        in_specs=(
            P(("dp", "table"), None),
            P(("dp", "table"), None),
            P(("dp", "table"), None),
            P("table", None, None),
            P("table", "dp"),
            P("table", "dp"),
            P("table", "dp"),
            P("table"),
            P(("dp", "table"), None, None),
            P(("dp", "table"), None, None),
        ),
        out_specs=(P("table", "dp"), P("table", "dp"), P("table", "dp"), P()),
        check_vma=False,
    )
```

```python
import jax
import jax.numpy as jnp
from jax import lax
from jax.experimental import pallas as pl
from jax.experimental.pallas import tpu as pltpu
from jax.sharding import PartitionSpec as P

AXES = ("dp", "table")
ROLES = (("x", "y", "z"), ("y", "z", "x"))
BF = jnp.bfloat16
F32 = jnp.float32


def coords(i):
    dp, table = i // 16, i % 16
    return {"x": dp // 2, "core": dp % 2, "y": table // 4, "z": table % 4}


def index_of(c):
    return (c["x"] * 2 + c["core"]) * 16 + c["y"] * 4 + c["z"]


def ring(role, shift):
    pairs = []
    for i in range(128):
        c = coords(i)
        axis = ROLES[c["core"]][role]
        c[axis] = (c[axis] + shift) % 4
        pairs.append((i, index_of(c)))
    return pairs


SWAP = [(i, i ^ 16) for i in range(128)]


def send(value, pairs):
    return lax.ppermute(value, AXES, pairs)


def in_hbm(value):
    return pltpu.with_memory_space_constraint(value, pltpu.HBM)


BESIDE_TRANSFER = pl.CostEstimate(flops=10**11, bytes_accessed=0, transcendentals=0)


def first_kernel(pos_ref, weight_ref, low_ref, high_ref, out_ref, mix_ref):
    slots, tokens = pos_ref.shape
    rows = mix_ref.shape[0]
    step = 64

    @pl.when(pl.program_id(0) == 0)
    def _():
        def block(b, carry):
            base = pl.multiple_of(b * step, step)
            place = lax.broadcasted_iota(jnp.int32, (step, tokens), 0) + base
            total = jnp.zeros((step, tokens), F32)
            for j in range(slots):
                hit = pos_ref[j : j + 1, :] == place
                total = total + jnp.where(hit, weight_ref[j : j + 1, :], 0.0)
            mix_ref[pl.ds(base, step), :] = total.astype(BF)
            return carry

        lax.fori_loop(0, rows // step, block, 0)

    next_kernel(None, mix_ref, low_ref, high_ref, out_ref)


def next_kernel(after_ref, mix_ref, low_ref, high_ref, out_ref):
    half = out_ref.shape[0] // 2
    for k, grad_ref in enumerate((low_ref, high_ref)):
        product = jnp.dot(mix_ref[...], grad_ref[...], preferred_element_type=F32)
        out_ref[k * half : (k + 1) * half] = product.astype(BF).reshape(half, *out_ref.shape[1:])


def combine(after, slot_pos, slot_weight, grad_out, mix, n_data, n_table, cap, start, w):
    tokens, width = grad_out.shape
    rows = n_table * cap
    blocks = width // n_data // w
    slots = pl.BlockSpec((slot_pos.shape[1], tokens), lambda i: (0, 0))
    mixed = pl.BlockSpec((rows, tokens), lambda i: (0, 0))
    grads = [
        pl.BlockSpec((tokens, w), lambda i, half=half: (0, (2 * i + half) * blocks + start // w))
        for half in range(2)
    ]
    out_spec = pl.BlockSpec((2 * n_table, cap, w), lambda i: (i, 0, 0))
    out_shape = pltpu.HBM((n_data * n_table, cap, w), BF)
    params = pltpu.CompilerParams(vmem_limit_bytes=32 << 20)
    anywhere = pl.BlockSpec(memory_space=pl.ANY)
    if mix is None:
        return pl.pallas_call(
            first_kernel,
            grid=(n_data // 2,),
            in_specs=[slots, slots, *grads],
            out_specs=[out_spec, mixed],
            out_shape=[out_shape, pltpu.HBM((rows, tokens), BF)],
            compiler_params=params,
            name="combine_first",
        )(slot_pos.T, slot_weight.T, grad_out, grad_out)
    return pl.pallas_call(
        next_kernel,
        grid=(n_data // 2,),
        in_specs=[anywhere, mixed, *grads],
        out_specs=out_spec,
        out_shape=out_shape,
        compiler_params=params,
        name="combine_next",
    )(after, mix, grad_out, grad_out)


def partials_kernel(place_ref, score_ref, query_ref, own_ref, other_ref):
    score = score_ref[...].reshape(-1, score_ref.shape[2])
    query = query_ref[...].reshape(-1, query_ref.shape[2]).astype(F32)
    parity = lax.broadcasted_iota(jnp.int32, query.shape, 0) & 1
    own = jnp.where(parity == place_ref[0], query, 0.0)
    both = jnp.concatenate([own, query - own], axis=1).astype(BF)
    product = lax.dot_general(
        score, both, (((0,), (0,)), ((), ())), preferred_element_type=F32
    ).astype(BF)
    own_ref[0] = product[:, : own_ref.shape[2]]
    other_ref[0] = product[:, own_ref.shape[2] :]


def partials(places, score, query):
    tokens, halves, keys = score.shape
    depth = query.shape[2]
    rows = keys // 4
    shape = jax.ShapeDtypeStruct((4, rows, depth), BF)
    return pl.pallas_call(
        partials_kernel,
        grid_spec=pltpu.PrefetchScalarGridSpec(
            num_scalar_prefetch=1,
            grid=(4,),
            in_specs=[
                pl.BlockSpec((tokens, halves, rows), lambda i, p: (0, 0, i)),
                pl.BlockSpec((tokens, halves, depth), lambda i, p: (0, 0, 0)),
            ],
            out_specs=[
                pl.BlockSpec((1, rows, depth), lambda i, p: ((i - p[1] + 4) % 4, 0, 0)),
                pl.BlockSpec((1, rows, depth), lambda i, p: ((i - p[3] + 4) % 4, 0, 0)),
            ],
        ),
        out_shape=[shape] * 2,
        compiler_params=pltpu.CompilerParams(vmem_limit_bytes=32 << 20),
        name="partials",
    )(places, score, in_hbm(query))


def merge_kernel(own_ref, got_ref, *out_refs):
    for r, out_ref in enumerate(out_refs):
        out_ref[...] = (own_ref[r].astype(F32) + got_ref[r].astype(F32)).astype(BF)


def merge(own, got):
    return pl.pallas_call(
        merge_kernel,
        out_shape=[jax.ShapeDtypeStruct(own.shape[1:], BF)] * 4,
        compiler_params=pltpu.CompilerParams(vmem_limit_bytes=32 << 20),
        name="merge",
    )(own, got)


def sum_kernel(a_ref, b_ref, c_ref, d_ref, out_ref):
    near = a_ref[...].astype(F32) + c_ref[...].astype(F32)
    far = b_ref[...].astype(F32) + d_ref[...].astype(F32)
    out_ref[...] = (near + far).astype(BF)


def sum_chunks(chunks):
    return pl.pallas_call(
        sum_kernel,
        out_shape=pltpu.HBM(chunks[0].shape, BF),
        cost_estimate=BESIDE_TRANSFER,
        compiler_params=pltpu.CompilerParams(vmem_limit_bytes=32 << 20),
        name="sum_chunks",
    )(*chunks)


def add_four(chunks):
    near = chunks[0].astype(F32) + chunks[2].astype(F32)
    return (near + (chunks[1].astype(F32) + chunks[3].astype(F32))).astype(BF)


def place_kernel(place_ref, *refs):
    blocks = refs[:4]
    out_ref, held, sem_in, sem_out = refs[-4:]
    rows = held.shape[1]
    loads = [pltpu.make_async_copy(blocks[k], held.at[k], sem_in.at[k]) for k in range(4)]
    for load in loads:
        load.start()
    stores = []
    for k in range(4):
        loads[k].wait()
        start = pl.multiple_of((place_ref[1] + k) % 4 * rows, rows)
        store = pltpu.make_async_copy(
            held.at[k], out_ref.at[place_ref[0], pl.ds(start, rows)], sem_out.at[k]
        )
        store.start()
        stores.append(store)
    for store in stores:
        store.wait()


def place_half(place, buffers, out=()):
    return pl.pallas_call(
        place_kernel,
        in_specs=[pl.BlockSpec(memory_space=pltpu.SMEM)]
        + [pl.BlockSpec(memory_space=pl.ANY)] * (4 + len(out)),
        out_specs=pl.BlockSpec(memory_space=pl.ANY),
        out_shape=jax.ShapeDtypeStruct((2, 4096, 256), BF),
        input_output_aliases={5: 0} if out else {},
        scratch_shapes=[
            pltpu.VMEM((4, *buffers[0].shape), BF),
            pltpu.SemaphoreType.DMA((4,)),
            pltpu.SemaphoreType.DMA((4,)),
        ],
        compiler_params=pltpu.CompilerParams(vmem_limit_bytes=16 << 20),
        name="place_half",
    )(place, *buffers, *out)


def adam_kernel(index_ref, steps_ref, *refs):
    rows = steps_ref.shape[2]
    slots = index_ref.shape[1]
    v_ref, m_ref, s_ref = refs[-6:-3] if len(refs) < 9 else refs[-9:-6]
    nv_ref, nm_ref, ns_ref = refs[-3:]
    arrived = refs[: len(refs) - (6 if len(refs) < 9 else 9)]
    base = pl.program_id(0) * rows
    place = lax.broadcasted_iota(jnp.int32, (rows, 128), 0).astype(F32).astype(BF)
    slot = (index_ref[...] - base).astype(F32).astype(BF)
    one, zero = jnp.ones((rows, 128), BF), jnp.zeros((rows, 128), BF)
    selector = jnp.concatenate(
        [jnp.where(slot[:, k : k + 128] == place, one, zero) for k in range(0, slots, 128)], axis=1
    )
    grad = [jnp.dot(selector, a[...], preferred_element_type=F32) for a in arrived]
    grad = grad[0] if len(grad) == 1 else jnp.concatenate(grad, axis=1)
    steps = steps_ref[0].astype(F32)
    first = 1.0 / (1.0 - jnp.exp(steps * jnp.log(jnp.float32(0.9))))
    second = 1.0 / (1.0 - jnp.exp(steps * jnp.log(jnp.float32(0.95))))
    first = jnp.broadcast_to(first, (128, rows)).T[:, :1]
    second = jnp.broadcast_to(second, (128, rows)).T[:, :1]
    new_first = 0.9 * m_ref[...] + 0.1 * grad
    new_second = 0.95 * s_ref[...] + 0.05 * grad * grad
    nm_ref[...] = new_first
    ns_ref[...] = new_second
    nv_ref[...] = v_ref[...] - 0.1 * (new_first * first) / (jnp.sqrt(new_second * second) + 1e-08)


def adam(index, steps, arrived, state, column, done=(), cost=None):
    owned = state[0].shape[0]
    rows = steps.shape[2]
    slots = index.shape[1]
    width = sum(a.shape[1] for a in arrived)
    block = pl.BlockSpec((rows, width), lambda i: (i, column))
    shape = jax.ShapeDtypeStruct(state[0].shape, F32)
    before = 2 + len(arrived) + 3
    return pl.pallas_call(
        adam_kernel,
        grid=(owned // rows,),
        in_specs=[
            pl.BlockSpec((1, slots), lambda i: (0, 0)),
            pl.BlockSpec((1, 1, rows), lambda i: (i, 0, 0)),
        ]
        + [pl.BlockSpec(a.shape, lambda i: (0, 0)) for a in arrived]
        + [block] * 3
        + [pl.BlockSpec(memory_space=pl.ANY)] * len(done),
        out_specs=[block] * 3,
        out_shape=[shape] * 3,
        input_output_aliases={before + k: k for k in range(len(done))},
        cost_estimate=cost,
        compiler_params=pltpu.CompilerParams(vmem_limit_bytes=40 << 20),
        name="adam",
    )(index, steps, *arrived, *[in_hbm(x) for x in state], *done)


def stack_kernel(*refs):
    for k, ref in enumerate(refs[:-1]):
        refs[-1][k] = ref[...]


def stack(blocks, cost=None):
    return pl.pallas_call(
        stack_kernel,
        out_shape=pltpu.HBM((len(blocks), *blocks[0].shape), BF),
        cost_estimate=cost,
        name="stack",
    )(*blocks)


def places_of():
    dp, table = lax.axis_index("dp"), lax.axis_index("table")
    at = {"x": dp // 2, "y": table // 4, "z": table % 4}
    core = dp % 2
    rows = []
    for c in (core, 1 - core):
        rows += [c, jnp.where(c == 0, at[ROLES[0][0]], at[ROLES[1][0]])]
    return jnp.stack(rows).astype(jnp.int32)


def per_device(
    grad_out,
    slot_weight,
    slot_pos,
    slot_rows,
    values,
    first_moment,
    second_moment,
    row_steps,
    queries,
    score_grad,
):
    n_table = lax.axis_size("table")
    n_data = lax.axis_size("dp")
    cap = slot_rows.shape[2]
    places = places_of()

    def exchange(ordered):
        moved = lax.all_to_all(ordered, AXES, split_axis=0, concat_axis=0, tiled=True)
        return moved.reshape(-1, moved.shape[2])

    own, other = partials(places, score_grad, queries)
    got = send(other, SWAP)
    sizes = (n_data, n_table, cap)
    ordered, mix = combine(None, slot_pos, slot_weight, grad_out, None, *sizes, 0, 256)
    chunks = merge(own, got)
    ordered, chunks = lax.optimization_barrier((ordered, chunks))
    chunks = [chunks[0]] + [send(chunks[r], ring(0, r)) for r in (1, 2, 3)]
    arrived = [exchange(ordered)]
    total = sum_chunks(chunks)
    total = add_four([total] + [send(total, ring(1, r)) for r in (1, 2, 3)])
    ordered = combine(total, slot_pos, slot_weight, grad_out, mix, *sizes, 256, 256)
    around = [total] + [send(total, ring(2, r)) for r in (1, 2, 3)]
    arrived.append(exchange(ordered))

    index = slot_rows.reshape(1, -1)
    steps = row_steps.reshape(-1, 1, 256)
    state = (values, first_moment, second_moment)
    outs = adam(index, steps, arrived[:1], state, 0)
    around, outs = lax.optimization_barrier((around, outs))
    final = sum_chunks(around)
    buffers = [final] + [send(final, ring(0, -r)) for r in (1, 2, 3)]
    outs = adam(index, steps, arrived[1:], state, 1, outs)
    buffers[1:], outs = lax.optimization_barrier((buffers[1:], outs))
    theirs = [send(b, SWAP) for b in buffers]
    subkey_out = place_half(places[:2], buffers)
    subkey_out = place_half(places[2:], theirs, (subkey_out,))
    return (*outs, subkey_out)


def solution(mesh):
    return jax.shard_map(
        per_device,
        mesh=mesh,
        in_specs=(
            P(("dp", "table"), None),
            P(("dp", "table"), None),
            P(("dp", "table"), None),
            P("table", None, None),
            P("table", "dp"),
            P("table", "dp"),
            P("table", "dp"),
            P("table"),
            P(("dp", "table"), None, None),
            P(("dp", "table"), None, None),
        ),
        out_specs=(P("table", "dp"), P("table", "dp"), P("table", "dp"), P()),
        check_vma=False,
    )
```
